128 devices in a mesh: tok: 128 (over y, z, x, core).
Axes of the slice: x: 4, y: 4, z: 4, core: 2. Of those that a mesh axis runs over, the one named last changes fastest.
Arguments:
- activations: bfloat16 [360448, 4096], P('tok'), may hold values from -70 to 70
- sketch: bfloat16 [4096, 128], replicated, may hold values from -0.09375 to 0.09375
Outputs:
- projection: float32 [4096, 128], replicated
The draws below stay inside these ranges and needn't reach their ends.
All inputs are finite; a program needn't handle non-finite values.
Results may differ from the reference program's by a relative error of at most 0.0003.
Values sent between devices are 32-bit elements; how exact they have to be, the bound alone decides.
A program may use at most 128 MiB of HBM per device.

```python
import math
import jax
import jax.numpy as jnp
from jax import lax

D = 4096
K = 128
ROWS_DEV = 2816
TOKENS = 360448
N_TOK = 128


def draw_activations(key, part):
    key = jax.random.fold_in(key, 11)
    first, second, third = jax.random.split(key, 3)
    where_row = jnp.arange(TOKENS, dtype=jnp.float32) / TOKENS
    row_scale = jnp.exp(jax.random.uniform(second, (TOKENS,), jnp.float32, math.log(0.5), math.log(1.5))) * jnp.exp(math.log(3.0) * where_row)
    col_scale = jnp.exp(jax.random.uniform(third, (D,), jnp.float32, math.log(0.3), math.log(3.0)))
    base = jnp.clip(jax.random.normal(first, (TOKENS, D), jnp.float32), -5.0, 5.0)
    return (base * row_scale[:, None] * col_scale[None, :]).astype(jnp.bfloat16)


def scatter_about(stream_key, dims, spread, bound, held_as=jnp.bfloat16):
    array = jax.random.normal(stream_key, dims, jnp.float32) * spread
    return jnp.minimum(jnp.maximum(array, -bound), bound).astype(held_as)


def setup_inputs(seed: int = 0) -> dict:
    streams_of = jax.random.split(jax.random.key(seed), 3)
    activations = draw_activations(jax.random.fold_in(streams_of[2], 71), 0)
    sketch = scatter_about(streams_of[1], (D, K), D ** -0.5, 0.09375)
    return dict(activations=activations, sketch=sketch)


def reference(activations, sketch):
    blocks = activations.reshape(N_TOK, ROWS_DEV, D)

    def sample_block(block):
        return jnp.dot(block.astype(jnp.float32), sketch.astype(jnp.float32), preferred_element_type=jnp.float32)
    sampled = lax.map(sample_block, blocks)

    def accumulate(total, pair):
        block, rows = pair
        term = lax.dot_general(block.astype(jnp.float32), rows.astype(jnp.bfloat16).astype(jnp.float32), (((0,), (0,)), ((), ())), preferred_element_type=jnp.float32)
        return (total + term, None)
    partial_value, _ = lax.scan(accumulate, jnp.zeros((D, K), jnp.float32), (blocks, sampled))
    flat = sampled.reshape(N_TOK * ROWS_DEV, K)
    gram_first = lax.dot_general(flat, flat, (((0,), (0,)), ((), ())), precision=lax.Precision.HIGHEST)
    upper_first = jnp.linalg.cholesky(gram_first).T
    basis_first = lax.linalg.triangular_solve(upper_first, flat, left_side=False, lower=False)
    gram_second = lax.dot_general(basis_first, basis_first, (((0,), (0,)), ((), ())), precision=lax.Precision.HIGHEST)
    upper_second = jnp.linalg.cholesky(gram_second).T
    factor = jnp.dot(upper_second, upper_first, precision=lax.Precision.HIGHEST)
    return lax.linalg.triangular_solve(factor, partial_value, left_side=False, lower=False)
```

```python
import functools

import jax
import jax.numpy as jnp
from jax import lax
from jax.experimental import pallas as pl
from jax.experimental.pallas import tpu as pltpu
from jax.sharding import PartitionSpec as P

MESH = pl.DeviceIdType.MESH
F32, BF16 = jnp.float32, jnp.bfloat16
NT = (((1,), (1,)), ((), ()))
TN = (((0,), (0,)), ((), ()))

D, K, ROWS = 4096, 128, 2816
HALF = D // 2
CHUNKS = (512, 512, 512, 512, 512, 256)
DEPTH = 2
SIZES = (768, 640, 640)
STARTS = (0, 768, 1408)
STRIDES = (2, 32, 8)
N_COPIES = 71


def split3(value):
    first = value.astype(BF16)
    rest = value - first.astype(F32)
    second = rest.astype(BF16)
    third = (rest - second.astype(F32)).astype(BF16)
    return first, second, third


def cholesky_blocks(remain, extra, inverse, low, high):
    sub = lax.broadcasted_iota(jnp.int32, (8, K), 0)

    def block_step(index, _):
        left, right = remain[0:8, :], extra[0:8, :]
        for j in range(8):
            column = jnp.broadcast_to(left[:, j : j + 1], (8, K))
            pivot = jnp.broadcast_to(column[j : j + 1, :], (8, K))
            scale = lax.rsqrt(pivot)
            scale = scale * (1.5 - 0.5 * pivot * scale * scale)
            left_row = jnp.broadcast_to(left[j : j + 1, :], (8, K)) * scale
            right_row = jnp.broadcast_to(right[j : j + 1, :], (8, K)) * scale
            factor = jnp.where(sub > j, column * scale, 0.0)
            left = jnp.where(sub == j, left_row, left - factor * left_row)
            right = jnp.where(sub == j, right_row, right - factor * right_row)
        inverse[pl.ds(pl.multiple_of(index * 8, 8), 8), :] = right
        both = jnp.concatenate([left, right], axis=1)
        one, two, three = (part.astype(F32) for part in split3(both))
        lhs = jnp.concatenate([one, one, two, two, one, three], axis=0)[:, :K].astype(BF16)
        rhs = jnp.concatenate([one, two, one, two, three, one], axis=0).astype(BF16)
        update = lax.dot_general(lhs, rhs, TN, preferred_element_type=F32)
        fresh = remain[...] - update[:, :K]
        remain[0 : K - 8, :] = pltpu.roll(fresh, K - 8, 1)[8:, :]
        remain[K - 8 :, :] = jnp.zeros((8, K), F32)
        extra[0 : K - 8, :] = extra[8:, :] - update[8:, K:]
        extra[K - 8 :, :] = jnp.zeros((8, K), F32)
        return 0

    lax.fori_loop(low, high, block_step, 0)


def main_kernel(
    a_hbm, s_hbm, o_hbm, w_ref,
    a, s, hl, outgo, income, half,
    r1a, r1b, r1c, s1a, s1b, s1c, r2a, r2b, r2c, r3a, r3b, r3c,
    whole, g_mine, g_core, g_one, g_two, g_three, g_full, g_extra, g_local,
    a_sem, s_sem, o_sem, send_sem, recv_sem,
):
    r1, s1, r2, r3 = (r1a, r1b, r1c), (s1a, s1b, s1c), (r2a, r2b, r2c), (r3a, r3b, r3c)
    me = lax.axis_index("tok")
    core = lax.rem(me, 2)
    partner = me + 1 - 2 * core
    place = [lax.rem(me // stride, 4) for stride in STRIDES]

    def at(axis, d):
        return lax.rem(place[axis] + d, 4)

    def device(axis, d):
        return me + (at(axis, d) - place[axis]) * STRIDES[axis]

    def rows(start, size):
        return pl.ds(pl.multiple_of(start, 8), size)

    starts = [sum(CHUNKS[:i]) for i in range(len(CHUNKS))]
    loads = [
        pltpu.make_async_copy(a_hbm.at[pl.ds(o, n)], a.at[pl.ds(o, n)], a_sem.at[i])
        for i, (o, n) in enumerate(zip(starts, CHUNKS))
    ]
    load_s = pltpu.make_async_copy(s_hbm, s, s_sem)
    load_s.start()
    for load in loads[:DEPTH]:
        load.start()

    barrier = pltpu.get_barrier_semaphore()
    pl.semaphore_signal(barrier, inc=1, device_id=(partner,), device_id_type=MESH)
    for axis in range(3):
        for d in (1, 2, 3):
            pl.semaphore_signal(barrier, inc=1, device_id=(device(axis, d),), device_id_type=MESH)

    sent = []

    def send(src, dst, target):
        i = len(sent)
        copy = pltpu.make_async_remote_copy(
            src_ref=src, dst_ref=dst, send_sem=send_sem.at[i], recv_sem=recv_sem.at[i],
            device_id=(target,), device_id_type=MESH,
        )
        copy.start()
        sent.append(copy)
        return copy

    load_s.wait()
    for i, (o, n) in enumerate(zip(starts, CHUNKS)):
        loads[i].wait()
        if i + DEPTH < len(loads):
            loads[i + DEPTH].start()
        sampled = jnp.dot(a[o : o + n, : D // 2], s[: D // 2, :], preferred_element_type=F32)
        sampled += jnp.dot(a[o : o + n, D // 2 :], s[D // 2 :, :], preferred_element_type=F32)
        turned = sampled.T
        high = turned.astype(BF16)
        hl[:K, o : o + n] = high
        hl[K:, o : o + n] = (turned - high.astype(F32)).astype(BF16)

    products = lax.dot_general(hl[...], hl[...], NT, preferred_element_type=F32)
    gram = (products[:K, :K] + products[K:, K:]) + (products[:K, K:] + products[K:, :K])
    g_local[...] = gram

    pl.semaphore_wait(barrier, 10)
    g_rows, g_other = rows(core * 64, 64), rows((1 - core) * 64, 64)
    g_copies = [send(g_local.at[g_other], g_core, partner)]

    def gram_stage(axis, slots, value):
        slots[place[axis]] = value
        mine = slots.at[place[axis]]
        return [send(mine, mine, device(axis, d)) for d in (1, 2, 3)]

    def gram_sum(copies, slots):
        for copy in copies:
            copy.wait_recv()
        return (slots[0] + slots[1]) + (slots[2] + slots[3])

    def columns(start, size):
        taken = a[:, pl.ds(pl.multiple_of(start, 128), size)]
        return jnp.dot(hl[:K, :], taken, preferred_element_type=F32).T

    to_core = []
    for j in range(3):
        piece = pl.ds(STARTS[j], SIZES[j])
        outgo[piece, :] = columns((1 - core) * HALF + STARTS[j], SIZES[j])
        to_core.append(send(outgo.at[piece], income.at[piece], partner))
        if j == 0:
            g_copies[0].wait_recv()
            g_copies = gram_stage(0, g_one, g_local[g_rows, :] + g_core[...])

    first = []
    for j in range(3):
        piece = pl.ds(STARTS[j], SIZES[j])
        quarter = SIZES[j] // 4
        value = columns(core * HALF + STARTS[j], SIZES[j])
        to_core[j].wait_recv()
        half[piece, :] = value + income[piece, :]
        first.append([
            send(half.at[rows(STARTS[j] + at(j, d) * quarter, quarter)], r1[j].at[d - 1], device(j, d))
            for d in (2, 1, 3)
        ])

    g_copies = gram_stage(1, g_two, gram_sum(g_copies, g_one))

    second = []
    for j in range(3):
        axis = (j + 1) % 3
        quarter, part = SIZES[j] // 4, SIZES[j] // 16
        for copy in first[j]:
            copy.wait_recv()
        s1[j][...] = (half[rows(STARTS[j] + place[j] * quarter, quarter), :] + r1[j][0]) + (r1[j][1] + r1[j][2])
        second.append([
            send(s1[j].at[rows(at(axis, d) * part, part)], r2[j].at[d - 1], device(axis, d))
            for d in (2, 1, 3)
        ])

    g_copies = gram_stage(2, g_three, gram_sum(g_copies, g_two))

    third = []
    for j in range(3):
        axis, last = (j + 1) % 3, (j + 2) % 3
        part = SIZES[j] // 16
        for copy in second[j]:
            copy.wait_recv()
        r3[j][place[last]] = (s1[j][rows(place[axis] * part, part), :] + r2[j][0]) + (r2[j][1] + r2[j][2])
        mine = r3[j].at[place[last]]
        third.append([send(mine, mine, device(last, d)) for d in (2, 1, 3)])

    g_mine[...] = gram_sum(g_copies, g_three)
    g_last = send(g_mine, g_full.at[g_rows], partner)
    g_full[g_rows, :] = g_mine[...]
    diagonal = lax.broadcasted_iota(jnp.int32, (K, K), 0) == lax.broadcasted_iota(jnp.int32, (K, K), 1)
    g_extra[...] = jnp.where(diagonal, 1.0, 0.0)
    g_last.wait_recv()
    cholesky_blocks(g_full, g_extra, w_ref, 0, 4)

    fourth = []
    for j in range(3):
        axis = (j + 1) % 3
        quarter, part = SIZES[j] // 4, SIZES[j] // 16
        for copy in third[j]:
            copy.wait_recv()
        here = rows(core * HALF + STARTS[j] + place[j] * quarter + place[axis] * part, part)
        whole[here, :] = (r3[j][0] + r3[j][1]) + (r3[j][2] + r3[j][3])
        fourth.append([send(whole.at[here], whole.at[here], device(axis, d)) for d in (2, 1, 3)])

    cholesky_blocks(g_full, g_extra, w_ref, 4, 10)

    fifth, forward = [], []
    for j in range(3):
        quarter = SIZES[j] // 4
        for copy in fourth[j]:
            copy.wait_recv()
        here = rows(core * HALF + STARTS[j] + place[j] * quarter, quarter)
        fifth.append([send(whole.at[here], whole.at[here], device(j, d)) for d in (2, 1, 3)])
        forward.append(send(whole.at[here], whole.at[here], partner))

    cholesky_blocks(g_full, g_extra, w_ref, 10, 16)

    for i, d in enumerate((2, 1, 3)):
        for j in (0, 1, 2):
            quarter = SIZES[j] // 4
            fifth[j][i].wait_recv()
            here = rows(core * HALF + STARTS[j] + at(j, 4 - d) * quarter, quarter)
            forward.append(send(whole.at[here], whole.at[here], partner))
    mine, other = rows(core * HALF, HALF), rows((1 - core) * HALF, HALF)
    out_mine = pltpu.make_async_copy(whole.at[mine], o_hbm.at[mine], o_sem.at[0])
    out_mine.start()
    for copy in forward:
        copy.wait_recv()
    out_other = pltpu.make_async_copy(whole.at[other], o_hbm.at[other], o_sem.at[1])
    out_other.start()
    for copy in sent:
        copy.wait_send()
    out_mine.wait()
    out_other.wait()


def apply_kernel(p_ref, w_ref, o_ref):
    p1, p2, p3 = split3(p_ref[...])
    w1, w2, w3 = (part.astype(F32).T.astype(BF16) for part in split3(w_ref[...]))
    wide = jnp.concatenate([w1, w2], axis=1)
    large = jnp.dot(
        jnp.concatenate([p1, p2], axis=1), jnp.concatenate([wide, wide], axis=0), preferred_element_type=F32
    )
    small = jnp.dot(
        jnp.concatenate([p1, p3], axis=1), jnp.concatenate([w3, w1], axis=0), preferred_element_type=F32
    )
    o_ref[...] = large[:, :K] + (large[:, K:] + small)


def local(activations, sketch):
    def slots(count, parts):
        return [pltpu.VMEM((count, size // parts, K), F32) for size in SIZES]

    partial, turned = pl.pallas_call(
        main_kernel,
        out_shape=[jax.ShapeDtypeStruct((D, K), F32), jax.ShapeDtypeStruct((K, K), F32)],
        in_specs=[pl.BlockSpec(memory_space=pl.ANY)] * 2,
        out_specs=[pl.BlockSpec(memory_space=pl.ANY), pl.BlockSpec(memory_space=pltpu.VMEM)],
        scratch_shapes=[
            pltpu.VMEM((ROWS, D), BF16),
            pltpu.VMEM((D, K), BF16),
            pltpu.VMEM((2 * K, ROWS), BF16),
            pltpu.VMEM((HALF, K), F32),
            pltpu.VMEM((HALF, K), F32),
            pltpu.VMEM((HALF, K), F32),
            *slots(3, 4),
            *[pltpu.VMEM((size // 4, K), F32) for size in SIZES],
            *slots(3, 16),
            *slots(4, 16),
            pltpu.VMEM((D, K), F32),
            pltpu.VMEM((64, K), F32),
            pltpu.VMEM((64, K), F32),
            pltpu.VMEM((4, 64, K), F32),
            pltpu.VMEM((4, 64, K), F32),
            pltpu.VMEM((4, 64, K), F32),
            pltpu.VMEM((K, K), F32),
            pltpu.VMEM((K, K), F32),
            pltpu.VMEM((K, K), F32),
            pltpu.SemaphoreType.DMA((len(CHUNKS),)),
            pltpu.SemaphoreType.DMA,
            pltpu.SemaphoreType.DMA((2,)),
            pltpu.SemaphoreType.DMA((N_COPIES,)),
            pltpu.SemaphoreType.DMA((N_COPIES,)),
        ],
        compiler_params=pltpu.CompilerParams(
            collective_id=0, has_side_effects=True, vmem_limit_bytes=48 * 2**20
        ),
    )(activations, sketch)
    tile = 1024
    return pl.pallas_call(
        apply_kernel,
        grid=(D // tile,),
        out_shape=jax.ShapeDtypeStruct((D, K), F32),
        in_specs=[pl.BlockSpec((tile, K), lambda i: (i, 0)), pl.BlockSpec((K, K), lambda i: (0, 0))],
        out_specs=pl.BlockSpec((tile, K), lambda i: (i, 0)),
        compiler_params=pltpu.CompilerParams(vmem_limit_bytes=32 * 2**20),
    )(partial, turned)


def solution(mesh):
    placed = (P("tok", None), P())
    return jax.shard_map(local, mesh=mesh, in_specs=placed, out_specs=P(), check_vma=False)
```

```python
import functools

import jax
import jax.numpy as jnp
from jax import lax
from jax.experimental import pallas as pl
from jax.experimental.pallas import tpu as pltpu
from jax.sharding import PartitionSpec as P

MESH = pl.DeviceIdType.MESH
F32, BF16 = jnp.float32, jnp.bfloat16
NT = (((1,), (1,)), ((), ()))
TN = (((0,), (0,)), ((), ()))

D, K, ROWS = 4096, 128, 2816
HALF = D // 2
CHUNKS = (256,) * 11
DEPTH = 3
SIZES = (768, 640, 640)
STARTS = (0, 768, 1408)
STRIDES = (2, 32, 8)
GRAM = ((0, 24), (24, 24), (48, 16))
N_COPIES = 89


def split3(value):
    first = value.astype(BF16)
    rest = value - first.astype(F32)
    second = rest.astype(BF16)
    third = (rest - second.astype(F32)).astype(BF16)
    return first, second, third


def cholesky_blocks(remain, extra, inverse, low, high):
    sub = lax.broadcasted_iota(jnp.int32, (8, K), 0)

    def block_step(index, _):
        left, right = remain[0:8, :], extra[0:8, :]

        def spread(value):
            return jnp.broadcast_to(value, (8, K))

        columns = [spread(left[:, j : j + 1]) for j in range(8)]
        block = {(i, j): spread(columns[j][i : i + 1, :]) for j in range(8) for i in range(j, 8)}
        lefts = [spread(left[i : i + 1, :]) for i in range(8)]
        rights = [spread(right[i : i + 1, :]) for i in range(8)]
        for j in range(8):
            pivot = block[j, j]
            scale = lax.rsqrt(pivot)
            scale = scale * (1.5 - 0.5 * pivot * scale * scale)
            factor = {i: block[i, j] * scale for i in range(j + 1, 8)}
            lefts[j], rights[j] = lefts[j] * scale, rights[j] * scale
            for i in range(j + 1, 8):
                for k in range(j + 1, i + 1):
                    block[i, k] = block[i, k] - factor[i] * factor[k]
                lefts[i] = lefts[i] - factor[i] * lefts[j]
                rights[i] = rights[i] - factor[i] * rights[j]
        left, right = lefts[0], rights[0]
        for j in range(1, 8):
            left = jnp.where(sub == j, lefts[j], left)
            right = jnp.where(sub == j, rights[j], right)
        inverse[pl.ds(pl.multiple_of(index * 8, 8), 8), :] = right
        both = jnp.concatenate([left, right], axis=1)
        one, two, three = (part.astype(F32) for part in split3(both))
        lhs = jnp.concatenate([one, one, two, two, one, three], axis=0)[:, :K].astype(BF16)
        rhs = jnp.concatenate([one, two, one, two, three, one], axis=0).astype(BF16)
        update = lax.dot_general(lhs, rhs, TN, preferred_element_type=F32)
        fresh = remain[...] - update[:, :K]
        remain[0 : K - 8, :] = pltpu.roll(fresh, K - 8, 1)[8:, :]
        remain[K - 8 :, :] = jnp.zeros((8, K), F32)
        extra[0 : K - 8, :] = extra[8:, :] - update[8:, K:]
        extra[K - 8 :, :] = jnp.zeros((8, K), F32)
        return 0

    lax.fori_loop(low, high, block_step, 0)


def main_kernel(
    a_hbm, s_hbm, whole, w_ref,
    a, s, hl, outgo, income, half,
    r1a, r1b, r1c, s1a, s1b, s1c, r2a, r2b, r2c, r3a, r3b, r3c,
    g_mine, g_core, g_one, g_two, g_three, g_full, g_extra, g_local,
    a_sem, s_sem, send_sem, recv_sem,
):
    r1, s1, r2, r3 = (r1a, r1b, r1c), (s1a, s1b, s1c), (r2a, r2b, r2c), (r3a, r3b, r3c)
    me = lax.axis_index("tok")
    core = lax.rem(me, 2)
    partner = me + 1 - 2 * core
    place = [lax.rem(me // stride, 4) for stride in STRIDES]

    def at(axis, d):
        return lax.rem(place[axis] + d, 4)

    def device(axis, d):
        return me + (at(axis, d) - place[axis]) * STRIDES[axis]

    def rows(start, size):
        return pl.ds(pl.multiple_of(start, 8), size)

    starts = [sum(CHUNKS[:i]) for i in range(len(CHUNKS))]
    loads = [
        pltpu.make_async_copy(a_hbm.at[pl.ds(o, n)], a.at[pl.ds(o, n)], a_sem.at[i])
        for i, (o, n) in enumerate(zip(starts, CHUNKS))
    ]
    load_s = pltpu.make_async_copy(s_hbm, s, s_sem)
    load_s.start()
    for load in loads[:DEPTH]:
        load.start()

    barrier = pltpu.get_barrier_semaphore()
    pl.semaphore_signal(barrier, inc=1, device_id=(partner,), device_id_type=MESH)
    for axis in range(3):
        for d in (1, 2, 3):
            pl.semaphore_signal(barrier, inc=1, device_id=(device(axis, d),), device_id_type=MESH)

    sent = []

    def send(src, dst, target):
        i = len(sent)
        copy = pltpu.make_async_remote_copy(
            src_ref=src, dst_ref=dst, send_sem=send_sem.at[i], recv_sem=recv_sem.at[i],
            device_id=(target,), device_id_type=MESH,
        )
        copy.start()
        sent.append(copy)
        return copy

    load_s.wait()
    for i, (o, n) in enumerate(zip(starts, CHUNKS)):
        loads[i].wait()
        if i + DEPTH < len(loads):
            loads[i + DEPTH].start()
        sampled = jnp.dot(a[o : o + n, : D // 2], s[: D // 2, :], preferred_element_type=F32)
        sampled += jnp.dot(a[o : o + n, D // 2 :], s[D // 2 :, :], preferred_element_type=F32)
        turned = sampled.T
        high = turned.astype(BF16)
        hl[:K, o : o + n] = high
        hl[K:, o : o + n] = (turned - high.astype(F32)).astype(BF16)

    products = lax.dot_general(hl[...], hl[...], NT, preferred_element_type=F32)
    gram = (products[:K, :K] + products[K:, K:]) + (products[:K, K:] + products[K:, :K])
    g_local[...] = gram

    pl.semaphore_wait(barrier, 10)
    g_rows, g_other = rows(core * 64, 64), rows((1 - core) * 64, 64)
    g_copies = [send(g_local.at[g_other], g_core, partner)]

    def gram_stage(stage, slots, value):
        copies = []
        for j, (start, size) in enumerate(GRAM):
            axis = (j + stage) % 3
            slots[place[axis], start : start + size, :] = value[start : start + size, :]
            mine = slots.at[place[axis], pl.ds(start, size)]
            copies += [send(mine, mine, device(axis, d)) for d in (2, 1, 3)]
        return copies

    def gram_sum(copies, slots):
        for copy in copies:
            copy.wait_recv()
        return (slots[0] + slots[1]) + (slots[2] + slots[3])

    def columns(start, size):
        taken = a[:, pl.ds(pl.multiple_of(start, 128), size)]
        return jnp.dot(hl[:K, :], taken, preferred_element_type=F32).T

    to_core = []
    for j in range(3):
        piece = pl.ds(STARTS[j], SIZES[j])
        outgo[piece, :] = columns((1 - core) * HALF + STARTS[j], SIZES[j])
        to_core.append(send(outgo.at[piece], income.at[piece], partner))
        if j == 0:
            g_copies[0].wait_recv()
            g_copies = gram_stage(0, g_one, g_local[g_rows, :] + g_core[...])

    first = []
    for j in range(3):
        piece = pl.ds(STARTS[j], SIZES[j])
        quarter = SIZES[j] // 4
        value = columns(core * HALF + STARTS[j], SIZES[j])
        to_core[j].wait_recv()
        half[piece, :] = value + income[piece, :]
        first.append([
            send(half.at[rows(STARTS[j] + at(j, d) * quarter, quarter)], r1[j].at[d - 1], device(j, d))
            for d in (2, 1, 3)
        ])

    g_copies = gram_stage(1, g_two, gram_sum(g_copies, g_one))

    second = []
    for j in range(3):
        axis = (j + 1) % 3
        quarter, part = SIZES[j] // 4, SIZES[j] // 16
        for copy in first[j]:
            copy.wait_recv()
        s1[j][...] = (half[rows(STARTS[j] + place[j] * quarter, quarter), :] + r1[j][0]) + (r1[j][1] + r1[j][2])
        second.append([
            send(s1[j].at[rows(at(axis, d) * part, part)], r2[j].at[d - 1], device(axis, d))
            for d in (2, 1, 3)
        ])

    g_copies = gram_stage(2, g_three, gram_sum(g_copies, g_two))

    third = []
    for j in range(3):
        axis, last = (j + 1) % 3, (j + 2) % 3
        part = SIZES[j] // 16
        for copy in second[j]:
            copy.wait_recv()
        r3[j][place[last]] = (s1[j][rows(place[axis] * part, part), :] + r2[j][0]) + (r2[j][1] + r2[j][2])
        mine = r3[j].at[place[last]]
        third.append([send(mine, mine, device(last, d)) for d in (2, 1, 3)])

    g_mine[...] = gram_sum(g_copies, g_three)
    g_last = send(g_mine, g_full.at[g_rows], partner)
    g_full[g_rows, :] = g_mine[...]
    diagonal = lax.broadcasted_iota(jnp.int32, (K, K), 0) == lax.broadcasted_iota(jnp.int32, (K, K), 1)
    g_extra[...] = jnp.where(diagonal, 1.0, 0.0)

    fourth = []
    for j in range(3):
        axis = (j + 1) % 3
        quarter, part = SIZES[j] // 4, SIZES[j] // 16
        for copy in third[j]:
            copy.wait_recv()
        here = rows(core * HALF + STARTS[j] + place[j] * quarter + place[axis] * part, part)
        whole[here, :] = (r3[j][0] + r3[j][1]) + (r3[j][2] + r3[j][3])
        fourth.append([send(whole.at[here], whole.at[here], device(axis, d)) for d in (2, 1, 3)])

    g_last.wait_recv()
    cholesky_blocks(g_full, g_extra, w_ref, 0, 7)

    fifth, forward = [], []
    for j in range(3):
        quarter = SIZES[j] // 4
        for copy in fourth[j]:
            copy.wait_recv()
        here = rows(core * HALF + STARTS[j] + place[j] * quarter, quarter)
        fifth.append([send(whole.at[here], whole.at[here], device(j, d)) for d in (2, 1, 3)])
        forward.append(send(whole.at[here], whole.at[here], partner))

    cholesky_blocks(g_full, g_extra, w_ref, 7, 16)

    for i, d in enumerate((2, 1, 3)):
        for j in (0, 1, 2):
            quarter = SIZES[j] // 4
            fifth[j][i].wait_recv()
            here = rows(core * HALF + STARTS[j] + at(j, 4 - d) * quarter, quarter)
            forward.append(send(whole.at[here], whole.at[here], partner))
    for copy in forward:
        copy.wait_recv()
    for copy in sent:
        copy.wait_send()


def apply_kernel(tile, p_ref, w_ref, o_hbm, out, o_sem):
    w1, w2, w3 = (part.astype(F32).T.astype(BF16) for part in split3(w_ref[...]))
    wide = jnp.concatenate([w1, w2], axis=1)
    large_w = jnp.concatenate([wide, wide], axis=0)
    small_w = jnp.concatenate([w3, w1], axis=0)
    copies = []
    for i in range(D // tile):
        piece = pl.ds(i * tile, tile)
        p1, p2, p3 = split3(p_ref[piece, :])
        large = jnp.dot(jnp.concatenate([p1, p2], axis=1), large_w, preferred_element_type=F32)
        small = jnp.dot(jnp.concatenate([p1, p3], axis=1), small_w, preferred_element_type=F32)
        out[piece, :] = large[:, :K] + (large[:, K:] + small)
        copies.append(pltpu.make_async_copy(out.at[piece], o_hbm.at[piece], o_sem.at[i]))
        copies[-1].start()
    for copy in copies:
        copy.wait()


def local(activations, sketch):
    def slots(count, parts):
        return [pltpu.VMEM((count, size // parts, K), F32) for size in SIZES]

    partial, turned = pl.pallas_call(
        main_kernel,
        out_shape=[jax.ShapeDtypeStruct((D, K), F32), jax.ShapeDtypeStruct((K, K), F32)],
        in_specs=[pl.BlockSpec(memory_space=pltpu.HBM)] * 2,
        out_specs=[pl.BlockSpec(memory_space=pltpu.VMEM)] * 2,
        scratch_shapes=[
            pltpu.VMEM((ROWS, D), BF16),
            pltpu.VMEM((D, K), BF16),
            pltpu.VMEM((2 * K, ROWS), BF16),
            pltpu.VMEM((HALF, K), F32),
            pltpu.VMEM((HALF, K), F32),
            pltpu.VMEM((HALF, K), F32),
            *slots(3, 4),
            *[pltpu.VMEM((size // 4, K), F32) for size in SIZES],
            *slots(3, 16),
            *slots(4, 16),
            pltpu.VMEM((64, K), F32),
            pltpu.VMEM((64, K), F32),
            pltpu.VMEM((4, 64, K), F32),
            pltpu.VMEM((4, 64, K), F32),
            pltpu.VMEM((4, 64, K), F32),
            pltpu.VMEM((K, K), F32),
            pltpu.VMEM((K, K), F32),
            pltpu.VMEM((K, K), F32),
            pltpu.SemaphoreType.DMA((len(CHUNKS),)),
            pltpu.SemaphoreType.DMA,
            pltpu.SemaphoreType.DMA((N_COPIES,)),
            pltpu.SemaphoreType.DMA((N_COPIES,)),
        ],
        compiler_params=pltpu.CompilerParams(
            collective_id=0, has_side_effects=True, vmem_limit_bytes=48 * 2**20
        ),
    )(activations, sketch)
    tile = 512
    return pl.pallas_call(
        functools.partial(apply_kernel, tile),
        out_shape=jax.ShapeDtypeStruct((D, K), F32),
        in_specs=[pl.BlockSpec(memory_space=pltpu.VMEM)] * 2,
        out_specs=pl.BlockSpec(memory_space=pltpu.HBM),
        scratch_shapes=[pltpu.VMEM((D, K), F32), pltpu.SemaphoreType.DMA((D // tile,))],
        compiler_params=pltpu.CompilerParams(vmem_limit_bytes=32 * 2**20),
    )(partial, turned)


def solution(mesh):
    placed = (P("tok", None), P())
    return jax.shard_map(local, mesh=mesh, in_specs=placed, out_specs=P(), check_vma=False)
```

```python
import functools

import jax
import jax.numpy as jnp
from jax import lax
from jax.experimental import pallas as pl
from jax.experimental.pallas import tpu as pltpu
from jax.sharding import PartitionSpec as P

MESH = pl.DeviceIdType.MESH
F32, BF16 = jnp.float32, jnp.bfloat16
NT = (((1,), (1,)), ((), ()))
TN = (((0,), (0,)), ((), ()))

D, K, ROWS = 4096, 128, 2816
HALF = D // 2
CHUNKS = (256,) * 11
DEPTH = 3
SIZES = (768, 768, 512)
STARTS = (0, 768, 1536)
STRIDES = (2, 32, 8)
GRAM = ((0, 24), (24, 24), (48, 16))
N_COPIES = 89


def split3(value):
    first = value.astype(BF16)
    rest = value - first.astype(F32)
    second = rest.astype(BF16)
    third = (rest - second.astype(F32)).astype(BF16)
    return first, second, third


def cholesky_blocks(remain, extra, inverse, low, high):
    sub = lax.broadcasted_iota(jnp.int32, (8, K), 0)

    def block_step(index, _):
        left, right = remain[0:8, :], extra[0:8, :]

        def spread(value):
            return jnp.broadcast_to(value, (8, K))

        columns = [spread(left[:, j : j + 1]) for j in range(8)]
        block = {(i, j): spread(columns[j][i : i + 1, :]) for j in range(8) for i in range(j, 8)}
        lefts = [spread(left[i : i + 1, :]) for i in range(8)]
        rights = [spread(right[i : i + 1, :]) for i in range(8)]
        for j in range(8):
            pivot = block[j, j]
            scale = lax.rsqrt(pivot)
            scale = scale * (1.5 - 0.5 * pivot * scale * scale)
            factor = {i: block[i, j] * scale for i in range(j + 1, 8)}
            lefts[j], rights[j] = lefts[j] * scale, rights[j] * scale
            for i in range(j + 1, 8):
                for k in range(j + 1, i + 1):
                    block[i, k] = block[i, k] - factor[i] * factor[k]
                lefts[i] = lefts[i] - factor[i] * lefts[j]
                rights[i] = rights[i] - factor[i] * rights[j]
        left, right = lefts[0], rights[0]
        for j in range(1, 8):
            left = jnp.where(sub == j, lefts[j], left)
            right = jnp.where(sub == j, rights[j], right)
        inverse[pl.ds(pl.multiple_of(index * 8, 8), 8), :] = right
        both = jnp.concatenate([left, right], axis=1)
        one, two, three = (part.astype(F32) for part in split3(both))
        lhs = jnp.concatenate([one, one, two, two, one, three], axis=0)[:, :K].astype(BF16)
        rhs = jnp.concatenate([one, two, one, two, three, one], axis=0).astype(BF16)
        update = lax.dot_general(lhs, rhs, TN, preferred_element_type=F32)
        fresh = remain[...] - update[:, :K]
        remain[0 : K - 8, :] = pltpu.roll(fresh, K - 8, 1)[8:, :]
        remain[K - 8 :, :] = jnp.zeros((8, K), F32)
        extra[0 : K - 8, :] = extra[8:, :] - update[8:, K:]
        extra[K - 8 :, :] = jnp.zeros((8, K), F32)
        return 0

    lax.fori_loop(low, high, block_step, 0)


def main_kernel(
    a_hbm, s, whole, w_ref,
    a, hl, outgo, income, half,
    r1a, r1b, r1c, s1a, s1b, s1c, r2a, r2b, r2c, r3a, r3b, r3c,
    g_mine, g_core, g_one, g_two, g_three, g_full, g_extra, g_local,
    a_sem, send_sem, recv_sem,
):
    r1, s1, r2, r3 = (r1a, r1b, r1c), (s1a, s1b, s1c), (r2a, r2b, r2c), (r3a, r3b, r3c)
    me = lax.axis_index("tok")
    core = lax.rem(me, 2)
    partner = me + 1 - 2 * core
    place = [lax.rem(me // stride, 4) for stride in STRIDES]

    def at(axis, d):
        return lax.rem(place[axis] + d, 4)

    def device(axis, d):
        return me + (at(axis, d) - place[axis]) * STRIDES[axis]

    def rows(start, size):
        return pl.ds(pl.multiple_of(start, 8), size)

    starts = [sum(CHUNKS[:i]) for i in range(len(CHUNKS))]
    loads = [
        pltpu.make_async_copy(a_hbm.at[pl.ds(o, n)], a.at[pl.ds(o, n)], a_sem.at[i])
        for i, (o, n) in enumerate(zip(starts, CHUNKS))
    ]
    for load in loads[:DEPTH]:
        load.start()

    barrier = pltpu.get_barrier_semaphore()
    pl.semaphore_signal(barrier, inc=1, device_id=(partner,), device_id_type=MESH)
    for axis in range(3):
        for d in (1, 2, 3):
            pl.semaphore_signal(barrier, inc=1, device_id=(device(axis, d),), device_id_type=MESH)

    sent = []

    def send(src, dst, target):
        i = len(sent)
        copy = pltpu.make_async_remote_copy(
            src_ref=src, dst_ref=dst, send_sem=send_sem.at[i], recv_sem=recv_sem.at[i],
            device_id=(target,), device_id_type=MESH,
        )
        copy.start()
        sent.append(copy)
        return copy

    for i, (o, n) in enumerate(zip(starts, CHUNKS)):
        loads[i].wait()
        if i + DEPTH < len(loads):
            loads[i + DEPTH].start()
        sampled = jnp.dot(a[o : o + n, : D // 2], s[: D // 2, :], preferred_element_type=F32)
        sampled += jnp.dot(a[o : o + n, D // 2 :], s[D // 2 :, :], preferred_element_type=F32)
        turned = sampled.T
        high = turned.astype(BF16)
        hl[:K, o : o + n] = high
        hl[K:, o : o + n] = (turned - high.astype(F32)).astype(BF16)

    products = lax.dot_general(hl[...], hl[...], NT, preferred_element_type=F32)
    gram = (products[:K, :K] + products[K:, K:]) + (products[:K, K:] + products[K:, :K])
    g_local[...] = gram

    pl.semaphore_wait(barrier, 10)
    g_rows, g_other = rows(core * 64, 64), rows((1 - core) * 64, 64)
    g_copies = [send(g_local.at[g_other], g_core, partner)]

    def gram_stage(stage, slots, value):
        copies = []
        for j, (start, size) in enumerate(GRAM):
            axis = (j + stage) % 3
            slots[place[axis], start : start + size, :] = value[start : start + size, :]
            mine = slots.at[place[axis], pl.ds(start, size)]
            copies += [send(mine, mine, device(axis, d)) for d in (2, 1, 3)]
        return copies

    def gram_sum(copies, slots):
        for copy in copies:
            copy.wait_recv()
        return (slots[0] + slots[1]) + (slots[2] + slots[3])

    def columns(start, size):
        taken = a[:, pl.ds(pl.multiple_of(start, 128), size)]
        return jnp.dot(hl[:K, :], taken, preferred_element_type=F32).T

    to_core, first = [], []

    def theirs(j):
        piece = pl.ds(STARTS[j], SIZES[j])
        outgo[piece, :] = columns((1 - core) * HALF + STARTS[j], SIZES[j])
        to_core.append(send(outgo.at[piece], income.at[piece], partner))

    def ours(j):
        piece = pl.ds(STARTS[j], SIZES[j])
        quarter = SIZES[j] // 4
        value = columns(core * HALF + STARTS[j], SIZES[j])
        to_core[j].wait_recv()
        half[piece, :] = value + income[piece, :]
        first.append([
            send(half.at[rows(STARTS[j] + at(j, d) * quarter, quarter)], r1[j].at[d - 1], device(j, d))
            for d in (2, 1, 3)
        ])

    theirs(0)
    g_copies[0].wait_recv()
    g_copies = gram_stage(0, g_one, g_local[g_rows, :] + g_core[...])
    theirs(1)
    ours(0)
    theirs(2)
    ours(1)
    ours(2)

    g_copies = gram_stage(1, g_two, gram_sum(g_copies, g_one))

    second = []
    for j in range(3):
        axis = (j + 1) % 3
        quarter, part = SIZES[j] // 4, SIZES[j] // 16
        for copy in first[j]:
            copy.wait_recv()
        s1[j][...] = (half[rows(STARTS[j] + place[j] * quarter, quarter), :] + r1[j][0]) + (r1[j][1] + r1[j][2])
        second.append([
            send(s1[j].at[rows(at(axis, d) * part, part)], r2[j].at[d - 1], device(axis, d))
            for d in (2, 1, 3)
        ])

    g_copies = gram_stage(2, g_three, gram_sum(g_copies, g_two))

    third = []
    for j in range(3):
        axis, last = (j + 1) % 3, (j + 2) % 3
        part = SIZES[j] // 16
        for copy in second[j]:
            copy.wait_recv()
        r3[j][place[last]] = (s1[j][rows(place[axis] * part, part), :] + r2[j][0]) + (r2[j][1] + r2[j][2])
        mine = r3[j].at[place[last]]
        third.append([send(mine, mine, device(last, d)) for d in (2, 1, 3)])

    g_mine[...] = gram_sum(g_copies, g_three)
    g_last = send(g_mine, g_full.at[g_rows], partner)
    g_full[g_rows, :] = g_mine[...]
    diagonal = lax.broadcasted_iota(jnp.int32, (K, K), 0) == lax.broadcasted_iota(jnp.int32, (K, K), 1)
    g_extra[...] = jnp.where(diagonal, 1.0, 0.0)

    fourth = []
    for j in range(3):
        axis = (j + 1) % 3
        quarter, part = SIZES[j] // 4, SIZES[j] // 16
        for copy in third[j]:
            copy.wait_recv()
        here = rows(core * HALF + STARTS[j] + place[j] * quarter + place[axis] * part, part)
        whole[here, :] = (r3[j][0] + r3[j][1]) + (r3[j][2] + r3[j][3])
        fourth.append([send(whole.at[here], whole.at[here], device(axis, d)) for d in (2, 1, 3)])

    g_last.wait_recv()
    cholesky_blocks(g_full, g_extra, w_ref, 0, 8)

    settled = len(sent)
    fifth, forward = [], []
    for j in range(3):
        quarter = SIZES[j] // 4
        for copy in fourth[j]:
            copy.wait_recv()
        here = rows(core * HALF + STARTS[j] + place[j] * quarter, quarter)
        fifth.append([send(whole.at[here], whole.at[here], device(j, d)) for d in (2, 1, 3)])
        forward.append(send(whole.at[here], whole.at[here], partner))

    cholesky_blocks(g_full, g_extra, w_ref, 8, 16)
    for copy in sent[:settled]:
        copy.wait_send()

    for i, d in enumerate((2, 1, 3)):
        for j in (0, 1, 2):
            quarter = SIZES[j] // 4
            fifth[j][i].wait_recv()
            here = rows(core * HALF + STARTS[j] + at(j, 4 - d) * quarter, quarter)
            forward.append(send(whole.at[here], whole.at[here], partner))
    for copy in forward:
        copy.wait_recv()
    for copy in sent[settled:]:
        copy.wait_send()


def apply_kernel(tile, p_ref, w_ref, o_hbm, out, o_sem):
    w1, w2, w3 = (part.astype(F32).T.astype(BF16) for part in split3(w_ref[...]))
    wide = jnp.concatenate([w1, w2], axis=1)
    large_w = jnp.concatenate([wide, wide], axis=0)
    small_w = jnp.concatenate([w3, w1], axis=0)
    copies = []
    for i in range(D // tile):
        piece = pl.ds(i * tile, tile)
        p1, p2, p3 = split3(p_ref[piece, :])
        large = jnp.dot(jnp.concatenate([p1, p2], axis=1), large_w, preferred_element_type=F32)
        small = jnp.dot(jnp.concatenate([p1, p3], axis=1), small_w, preferred_element_type=F32)
        out[piece, :] = large[:, :K] + (large[:, K:] + small)
        copies.append(pltpu.make_async_copy(out.at[piece], o_hbm.at[piece], o_sem.at[i]))
        copies[-1].start()
    for copy in copies:
        copy.wait()


def local(activations, sketch):
    def slots(count, parts):
        return [pltpu.VMEM((count, size // parts, K), F32) for size in SIZES]

    partial, turned = pl.pallas_call(
        main_kernel,
        out_shape=[jax.ShapeDtypeStruct((D, K), F32), jax.ShapeDtypeStruct((K, K), F32)],
        in_specs=[pl.BlockSpec(memory_space=pltpu.HBM), pl.BlockSpec(memory_space=pltpu.VMEM)],
        out_specs=[pl.BlockSpec(memory_space=pltpu.VMEM)] * 2,
        scratch_shapes=[
            pltpu.VMEM((ROWS, D), BF16),
            pltpu.VMEM((2 * K, ROWS), BF16),
            pltpu.VMEM((HALF, K), F32),
            pltpu.VMEM((HALF, K), F32),
            pltpu.VMEM((HALF, K), F32),
            *slots(3, 4),
            *[pltpu.VMEM((size // 4, K), F32) for size in SIZES],
            *slots(3, 16),
            *slots(4, 16),
            pltpu.VMEM((64, K), F32),
            pltpu.VMEM((64, K), F32),
            pltpu.VMEM((4, 64, K), F32),
            pltpu.VMEM((4, 64, K), F32),
            pltpu.VMEM((4, 64, K), F32),
            pltpu.VMEM((K, K), F32),
            pltpu.VMEM((K, K), F32),
            pltpu.VMEM((K, K), F32),
            pltpu.SemaphoreType.DMA((len(CHUNKS),)),
            pltpu.SemaphoreType.DMA((N_COPIES,)),
            pltpu.SemaphoreType.DMA((N_COPIES,)),
        ],
        compiler_params=pltpu.CompilerParams(
            collective_id=0, has_side_effects=True, vmem_limit_bytes=48 * 2**20
        ),
    )(activations, sketch)
    tile = 512
    return pl.pallas_call(
        functools.partial(apply_kernel, tile),
        out_shape=jax.ShapeDtypeStruct((D, K), F32),
        in_specs=[pl.BlockSpec(memory_space=pltpu.VMEM)] * 2,
        out_specs=pl.BlockSpec(memory_space=pltpu.HBM),
        scratch_shapes=[pltpu.VMEM((D, K), F32), pltpu.SemaphoreType.DMA((D // tile,))],
        compiler_params=pltpu.CompilerParams(vmem_limit_bytes=32 * 2**20),
    )(partial, turned)


def solution(mesh):
    placed = (P("tok", None), P())
    return jax.shard_map(local, mesh=mesh, in_specs=placed, out_specs=P(), check_vma=False)
```

```python
import functools

import jax
import jax.numpy as jnp
from jax import lax
from jax.experimental import pallas as pl
from jax.experimental.pallas import tpu as pltpu
from jax.sharding import PartitionSpec as P

MESH = pl.DeviceIdType.MESH
F32, BF16 = jnp.float32, jnp.bfloat16
NT = (((1,), (1,)), ((), ()))
TN = (((0,), (0,)), ((), ()))

D, K, ROWS = 4096, 128, 2816
HALF = D // 2
CHUNKS = (256,) * 11
DEPTH = 3
SIZES = (768, 768, 512)
STARTS = (0, 768, 1536)
STRIDES = (2, 32, 8)
GRAM = ((0, 24), (24, 24), (48, 16))
N_COPIES = 89


def split3(value):
    first = value.astype(BF16)
    rest = value - first.astype(F32)
    second = rest.astype(BF16)
    third = (rest - second.astype(F32)).astype(BF16)
    return first, second, third


def cholesky_blocks(remain, extra, inverse, low, high):
    sub = lax.broadcasted_iota(jnp.int32, (8, K), 0)

    def block_step(index, _):
        left, right = remain[0:8, :], extra[0:8, :]

        def spread(value):
            return jnp.broadcast_to(value, (8, K))

        columns = [spread(left[:, j : j + 1]) for j in range(8)]
        block = {(i, j): spread(columns[j][i : i + 1, :]) for j in range(8) for i in range(j, 8)}
        lefts = [spread(left[i : i + 1, :]) for i in range(8)]
        rights = [spread(right[i : i + 1, :]) for i in range(8)]
        for j in range(8):
            pivot = block[j, j]
            scale = lax.rsqrt(pivot)
            scale = scale * (1.5 - 0.5 * pivot * scale * scale)
            factor = {i: block[i, j] * scale for i in range(j + 1, 8)}
            lefts[j], rights[j] = lefts[j] * scale, rights[j] * scale
            for i in range(j + 1, 8):
                for k in range(j + 1, i + 1):
                    block[i, k] = block[i, k] - factor[i] * factor[k]
                lefts[i] = lefts[i] - factor[i] * lefts[j]
                rights[i] = rights[i] - factor[i] * rights[j]
        left, right = lefts[0], rights[0]
        for j in range(1, 8):
            left = jnp.where(sub == j, lefts[j], left)
            right = jnp.where(sub == j, rights[j], right)
        inverse[pl.ds(pl.multiple_of(index * 8, 8), 8), :] = right
        both = jnp.concatenate([left, right], axis=1)
        one, two, three = (part.astype(F32) for part in split3(both))
        lhs = jnp.concatenate([one, one, two, two, one, three], axis=0)[:, :K].astype(BF16)
        rhs = jnp.concatenate([one, two, one, two, three, one], axis=0).astype(BF16)
        update = lax.dot_general(lhs, rhs, TN, preferred_element_type=F32)
        fresh = remain[...] - update[:, :K]
        remain[0 : K - 8, :] = pltpu.roll(fresh, K - 8, 1)[8:, :]
        remain[K - 8 :, :] = jnp.zeros((8, K), F32)
        extra[0 : K - 8, :] = extra[8:, :] - update[8:, K:]
        extra[K - 8 :, :] = jnp.zeros((8, K), F32)
        return 0

    lax.fori_loop(low, high, block_step, 0)


def main_kernel(
    a_hbm, s, whole, w_ref,
    a, hl, outgo, income, half,
    r1a, r1b, r1c, s1a, s1b, s1c, r2a, r2b, r2c, r3a, r3b, r3c,
    g_mine, g_core, g_one, g_two, g_three, g_full, g_extra, g_local,
    a_sem, send_sem, recv_sem,
):
    r1, s1, r2, r3 = (r1a, r1b, r1c), (s1a, s1b, s1c), (r2a, r2b, r2c), (r3a, r3b, r3c)
    me = lax.axis_index("tok")
    core = lax.rem(me, 2)
    partner = me + 1 - 2 * core
    place = [lax.rem(me // stride, 4) for stride in STRIDES]

    def at(axis, d):
        return lax.rem(place[axis] + d, 4)

    def device(axis, d):
        return me + (at(axis, d) - place[axis]) * STRIDES[axis]

    def rows(start, size):
        return pl.ds(pl.multiple_of(start, 8), size)

    starts = [sum(CHUNKS[:i]) for i in range(len(CHUNKS))]
    loads = [
        pltpu.make_async_copy(a_hbm.at[pl.ds(o, n)], a.at[pl.ds(o, n)], a_sem.at[i])
        for i, (o, n) in enumerate(zip(starts, CHUNKS))
    ]
    for load in loads[:DEPTH]:
        load.start()

    barrier = pltpu.get_barrier_semaphore()
    pl.semaphore_signal(barrier, inc=1, device_id=(partner,), device_id_type=MESH)
    for axis in range(3):
        for d in (1, 2, 3):
            pl.semaphore_signal(barrier, inc=1, device_id=(device(axis, d),), device_id_type=MESH)

    sent = []

    def send(src, dst, target):
        i = len(sent)
        copy = pltpu.make_async_remote_copy(
            src_ref=src, dst_ref=dst, send_sem=send_sem.at[i], recv_sem=recv_sem.at[i],
            device_id=(target,), device_id_type=MESH,
        )
        copy.start()
        sent.append(copy)
        return copy

    for i, (o, n) in enumerate(zip(starts, CHUNKS)):
        loads[i].wait()
        if i + DEPTH < len(loads):
            loads[i + DEPTH].start()
        sampled = jnp.dot(a[o : o + n, : D // 2], s[: D // 2, :], preferred_element_type=F32)
        sampled += jnp.dot(a[o : o + n, D // 2 :], s[D // 2 :, :], preferred_element_type=F32)
        turned = sampled.T
        high = turned.astype(BF16)
        hl[:K, o : o + n] = high
        hl[K:, o : o + n] = (turned - high.astype(F32)).astype(BF16)

    products = lax.dot_general(hl[...], hl[...], NT, preferred_element_type=F32)
    gram = (products[:K, :K] + products[K:, K:]) + (products[:K, K:] + products[K:, :K])
    g_local[...] = gram

    pl.semaphore_wait(barrier, 10)
    g_rows, g_other = rows(core * 64, 64), rows((1 - core) * 64, 64)
    g_copies = [send(g_local.at[g_other], g_core, partner)]

    def gram_stage(stage, slots, value):
        copies = []
        for j, (start, size) in enumerate(GRAM):
            axis = (j + stage) % 3
            slots[place[axis], start : start + size, :] = value[start : start + size, :]
            mine = slots.at[place[axis], pl.ds(start, size)]
            copies += [send(mine, mine, device(axis, d)) for d in (2, 1, 3)]
        return copies

    def gram_sum(copies, slots):
        for copy in copies:
            copy.wait_recv()
        return (slots[0] + slots[1]) + (slots[2] + slots[3])

    def columns(start, size):
        taken = a[:, pl.ds(pl.multiple_of(start, 128), size)]
        return jnp.dot(hl[:K, :], taken, preferred_element_type=F32).T

    to_core, first = [], []

    def theirs(j):
        piece = pl.ds(STARTS[j], SIZES[j])
        outgo[piece, :] = columns((1 - core) * HALF + STARTS[j], SIZES[j])
        to_core.append(send(outgo.at[piece], income.at[piece], partner))

    def ours(j):
        piece = pl.ds(STARTS[j], SIZES[j])
        quarter = SIZES[j] // 4
        value = columns(core * HALF + STARTS[j], SIZES[j])
        to_core[j].wait_recv()
        half[piece, :] = value + income[piece, :]
        first.append([
            send(half.at[rows(STARTS[j] + at(j, d) * quarter, quarter)], r1[j].at[d - 1], device(j, d))
            for d in (2, 1, 3)
        ])

    theirs(0)
    g_copies[0].wait_recv()
    g_copies = gram_stage(0, g_one, g_local[g_rows, :] + g_core[...])
    theirs(1)
    ours(0)
    theirs(2)
    ours(1)
    ours(2)

    g_copies = gram_stage(1, g_two, gram_sum(g_copies, g_one))

    second = []
    for j in range(3):
        axis = (j + 1) % 3
        quarter, part = SIZES[j] // 4, SIZES[j] // 16
        for copy in first[j]:
            copy.wait_recv()
        s1[j][...] = (half[rows(STARTS[j] + place[j] * quarter, quarter), :] + r1[j][0]) + (r1[j][1] + r1[j][2])
        second.append([
            send(s1[j].at[rows(at(axis, d) * part, part)], r2[j].at[d - 1], device(axis, d))
            for d in (2, 1, 3)
        ])

    g_copies = gram_stage(2, g_three, gram_sum(g_copies, g_two))

    third = []
    for j in range(3):
        axis, last = (j + 1) % 3, (j + 2) % 3
        part = SIZES[j] // 16
        for copy in second[j]:
            copy.wait_recv()
        r3[j][place[last]] = (s1[j][rows(place[axis] * part, part), :] + r2[j][0]) + (r2[j][1] + r2[j][2])
        mine = r3[j].at[place[last]]
        third.append([send(mine, mine, device(last, d)) for d in (2, 1, 3)])

    g_mine[...] = gram_sum(g_copies, g_three)
    g_last = send(g_mine, g_full.at[g_rows], partner)
    g_full[g_rows, :] = g_mine[...]
    diagonal = lax.broadcasted_iota(jnp.int32, (K, K), 0) == lax.broadcasted_iota(jnp.int32, (K, K), 1)
    g_extra[...] = jnp.where(diagonal, 1.0, 0.0)

    fourth = []
    for j in range(3):
        axis = (j + 1) % 3
        quarter, part = SIZES[j] // 4, SIZES[j] // 16
        for copy in third[j]:
            copy.wait_recv()
        here = rows(core * HALF + STARTS[j] + place[j] * quarter + place[axis] * part, part)
        whole[here, :] = (r3[j][0] + r3[j][1]) + (r3[j][2] + r3[j][3])
        fourth.append([send(whole.at[here], whole.at[here], device(axis, d)) for d in (2, 1, 3)])

    g_last.wait_recv()
    cholesky_blocks(g_full, g_extra, w_ref, 0, 8)

    settled = len(sent)
    fifth, forward = [], []
    for j in range(3):
        quarter = SIZES[j] // 4
        for copy in fourth[j]:
            copy.wait_recv()
        here = rows(core * HALF + STARTS[j] + place[j] * quarter, quarter)
        fifth.append([send(whole.at[here], whole.at[here], device(j, d)) for d in (2, 1, 3)])
        forward.append(send(whole.at[here], whole.at[here], partner))

    cholesky_blocks(g_full, g_extra, w_ref, 8, 16)
    for copy in sent[:settled]:
        copy.wait_send()

    for i, d in ((1, 1), (2, 3), (0, 2)):
        for j in (0, 1, 2):
            quarter = SIZES[j] // 4
            fifth[j][i].wait_recv()
            here = rows(core * HALF + STARTS[j] + at(j, 4 - d) * quarter, quarter)
            forward.append(send(whole.at[here], whole.at[here], partner))
    for copy in forward:
        copy.wait_recv()
    for copy in sent[settled:]:
        copy.wait_send()


def apply_kernel(tile, p_ref, w_ref, o_hbm, out, o_sem):
    w1, w2, w3 = (part.astype(F32).T.astype(BF16) for part in split3(w_ref[...]))
    wide = jnp.concatenate([w1, w2], axis=1)
    large_w = jnp.concatenate([wide, wide], axis=0)
    small_w = jnp.concatenate([w3, w1], axis=0)
    copies = []
    for i in range(D // tile):
        piece = pl.ds(i * tile, tile)
        p1, p2, p3 = split3(p_ref[piece, :])
        large = jnp.dot(jnp.concatenate([p1, p2], axis=1), large_w, preferred_element_type=F32)
        small = jnp.dot(jnp.concatenate([p1, p3], axis=1), small_w, preferred_element_type=F32)
        out[piece, :] = large[:, :K] + (large[:, K:] + small)
        copies.append(pltpu.make_async_copy(out.at[piece], o_hbm.at[piece], o_sem.at[i]))
        copies[-1].start()
    for copy in copies:
        copy.wait()


def local(activations, sketch):
    def slots(count, parts):
        return [pltpu.VMEM((count, size // parts, K), F32) for size in SIZES]

    partial, turned = pl.pallas_call(
        main_kernel,
        out_shape=[jax.ShapeDtypeStruct((D, K), F32), jax.ShapeDtypeStruct((K, K), F32)],
        in_specs=[pl.BlockSpec(memory_space=pltpu.HBM), pl.BlockSpec(memory_space=pltpu.VMEM)],
        out_specs=[pl.BlockSpec(memory_space=pltpu.VMEM)] * 2,
        scratch_shapes=[
            pltpu.VMEM((ROWS, D), BF16),
            pltpu.VMEM((2 * K, ROWS), BF16),
            pltpu.VMEM((HALF, K), F32),
            pltpu.VMEM((HALF, K), F32),
            pltpu.VMEM((HALF, K), F32),
            *slots(3, 4),
            *[pltpu.VMEM((size // 4, K), F32) for size in SIZES],
            *slots(3, 16),
            *slots(4, 16),
            pltpu.VMEM((64, K), F32),
            pltpu.VMEM((64, K), F32),
            pltpu.VMEM((4, 64, K), F32),
            pltpu.VMEM((4, 64, K), F32),
            pltpu.VMEM((4, 64, K), F32),
            pltpu.VMEM((K, K), F32),
            pltpu.VMEM((K, K), F32),
            pltpu.VMEM((K, K), F32),
            pltpu.SemaphoreType.DMA((len(CHUNKS),)),
            pltpu.SemaphoreType.DMA((N_COPIES,)),
            pltpu.SemaphoreType.DMA((N_COPIES,)),
        ],
        compiler_params=pltpu.CompilerParams(
            collective_id=0, has_side_effects=True, vmem_limit_bytes=48 * 2**20
        ),
    )(activations, sketch)
    tile = 512
    return pl.pallas_call(
        functools.partial(apply_kernel, tile),
        out_shape=jax.ShapeDtypeStruct((D, K), F32),
        in_specs=[pl.BlockSpec(memory_space=pltpu.VMEM)] * 2,
        out_specs=pl.BlockSpec(memory_space=pltpu.HBM),
        scratch_shapes=[pltpu.VMEM((D, K), F32), pltpu.SemaphoreType.DMA((D // tile,))],
        compiler_params=pltpu.CompilerParams(vmem_limit_bytes=32 * 2**20),
    )(partial, turned)


def solution(mesh):
    placed = (P("tok", None), P())
    return jax.shard_map(local, mesh=mesh, in_specs=placed, out_specs=P(), check_vma=False)
```
